1024 devices in a mesh: row: 32 (over x, y, core), col: 32 (over z).
Axes of the slice: x: 4, y: 4, z: 32, core: 2. Of those that a mesh axis runs over, the one named last changes fastest.
Arguments:
- values: bfloat16 [32, 32, 10, 64, 64], P('row', 'col'), may hold values from -0.59765625 to 0.59765625
- block_rows: int32 [32, 32, 10], P('row', 'col'), may hold values from -1 to 1279, as said below
- block_cols: int32 [32, 32, 10], P('row', 'col'), may hold values from -1 to 1279, as said below
Outputs:
- purified: float32 [32, 32, 10, 64, 64], P('row', 'col')
The draws below stay inside these ranges and needn't reach their ends.
Inputs may be any that keep to these rules, and one draw needn't show every extreme that they name: `block_rows`: tile (i, j) holds only blocks whose row lies in [i * 40, (i + 1) * 40) and whose column lies in [j * 40, (j + 1) * 40); live slots come first and empty ones hold -1; no block is stored twice; a block row holds at most 7 blocks. `block_cols`: empty slots hold -1 here exactly where block_rows does.
All inputs are finite; a program needn't handle non-finite values.
Results may differ from the reference program's by a relative error of at most 0.0021.
Values may be sent and summed in bfloat16 or wider, within the bound.
A program may use at most 32 MiB of HBM per device.

```python
import jax
import jax.numpy as jnp
from jax import lax

BLK = 64
BROWS = 40
NEIGH = 7
CAP = 10
NBLOCKS = 1280
COL_SPAN = 40
N_ROW = 32
N_COL = 32


def block_pattern(key):
    total = NBLOCKS * NEIGH
    shuffle = jax.random.permutation(jax.random.fold_in(key, 101), NBLOCKS).astype(jnp.int32)
    entry = jnp.arange(total, dtype=jnp.int32)
    anchor = entry // NEIGH
    offset = entry % NEIGH - NEIGH // 2
    row_ids = shuffle[anchor]
    col_ids = shuffle[(anchor + offset) % NBLOCKS]
    tiles = row_ids // BROWS * N_COL + col_ids // COL_SPAN
    priority = jax.random.permutation(jax.random.fold_in(key, 102), total).astype(jnp.int32)
    order = jnp.argsort(tiles * total + priority, stable=True)
    sorted_tiles = tiles[order]
    starts = jnp.searchsorted(sorted_tiles, sorted_tiles, side='left').astype(jnp.int32)
    ranks = entry - starts
    slots = N_ROW * N_COL * CAP
    target = jnp.where(ranks < CAP, sorted_tiles * CAP + ranks, slots)
    rows_out = jnp.full((slots,), -1, jnp.int32).at[target].set(row_ids[order], mode='drop')
    cols_out = jnp.full((slots,), -1, jnp.int32).at[target].set(col_ids[order], mode='drop')
    return (rows_out.reshape(N_ROW, N_COL, CAP), cols_out.reshape(N_ROW, N_COL, CAP))


def draw_block_rows(key, part):
    rows_out, cols_out = block_pattern(key)
    return rows_out


def draw_block_cols(key, part):
    rows_out, cols_out = block_pattern(key)
    return cols_out


def steps_of(stream_key, dims, shards, least, largest):
    def one(position, parts):
        draws = jax.random.uniform(jax.random.fold_in(jax.random.fold_in(stream_key, 6), position), (parts,), jnp.float32, least / len(shards), largest / len(shards))
        return jnp.repeat(jnp.exp(draws), dims[position] // parts).reshape((-1,) + (1,) * (len(dims) - position - 1))

    factor_of = one(*shards[0])
    for cut in shards[1:]:
        factor_of = factor_of * one(*cut)
    return factor_of


def scatter_about(own_key, shape, spread, bound, pieces=(), held_as=jnp.bfloat16):
    array = spread * jax.random.normal(own_key, shape, jnp.float32)
    if pieces:
        array = array * steps_of(own_key, shape, pieces, -0.22, 0.18)
    return jnp.clip(array, -bound, bound).astype(held_as)


def setup_inputs(seed: int = 0) -> dict:
    seeds = jax.random.split(jax.random.key(seed), 4)
    return {
        "values": scatter_about(seeds[0], (N_ROW, N_COL, CAP, BLK, BLK), 0.1, 0.59765625, ((0, 32), (1, 32))),
        "block_rows": draw_block_rows(jax.random.fold_in(seeds[3], 71), 0),
        "block_cols": draw_block_cols(jax.random.fold_in(seeds[3], 71), 0),
    }


def select_pairs(left_rows, left_cols, right_rows, right_cols, out_rows, out_cols):
    left_count = left_rows.shape[0]
    right_count = right_rows.shape[0]
    same_row = (left_rows[None, :] == out_rows[:, None]) & (left_rows[None, :] >= 0)
    linked = (right_rows[None, None, :] == left_cols[None, :, None]) & (right_cols[None, None, :] == out_cols[:, None, None]) & (right_rows[None, None, :] >= 0)
    found = jnp.any(linked, axis=2)
    partner = jnp.sum(jnp.where(linked, jnp.arange(right_count, dtype=jnp.int32)[None, None, :], 0), axis=2).astype(jnp.int32)
    valid = same_row & found
    scores = jnp.where(valid, left_count - jnp.arange(left_count, dtype=jnp.int32)[None, :], 0).astype(jnp.int32)
    top_scores, chosen = lax.top_k(scores, min(NEIGH, left_count))
    chosen = chosen.astype(jnp.int32)
    paired = jnp.take_along_axis(partner, chosen, axis=1).astype(jnp.int32)
    return chosen, paired, top_scores > 0


def block_product(left_sel, right_sel, keep):
    left_wide = jnp.where(keep[:, :, None, None], left_sel.astype(jnp.float32), 0.0)
    return jnp.einsum("opik,opkj->oij", left_wide, right_sel.astype(jnp.float32))


def reference(values, block_rows, block_cols):
    tile_total = N_ROW * N_COL

    def square_tile(index):
        row_owner = index // N_COL
        col_owner = index % N_COL
        panel_vals = values[row_owner].reshape(N_COL * CAP, BLK, BLK)
        panel_rows = block_rows[row_owner].reshape(-1)
        panel_cols = block_cols[row_owner].reshape(-1)
        column_vals = values[:, col_owner].reshape(N_ROW * CAP, BLK, BLK)
        column_rows = block_rows[:, col_owner].reshape(-1)
        column_cols = block_cols[:, col_owner].reshape(-1)
        tile_rows = block_rows[row_owner, col_owner]
        tile_cols = block_cols[row_owner, col_owner]
        chosen, paired, keep = select_pairs(panel_rows, panel_cols, column_rows, column_cols, tile_rows, tile_cols)
        square = block_product(panel_vals[chosen], column_vals[paired], keep)
        return square, chosen, paired, keep

    squares, chosen_all, paired_all, keep_all = lax.map(square_tile, jnp.arange(tile_total, dtype=jnp.int32))
    square_sent = squares.astype(jnp.bfloat16).reshape(N_ROW, N_COL, CAP, BLK, BLK)

    def cube_tile(packed):
        index, chosen, paired, keep = packed
        row_owner = index // N_COL
        col_owner = index % N_COL
        panel_square = square_sent[row_owner].reshape(N_COL * CAP, BLK, BLK)
        column_vals = values[:, col_owner].reshape(N_ROW * CAP, BLK, BLK)
        return block_product(panel_square[chosen], column_vals[paired], keep)

    cubes = lax.map(cube_tile, (jnp.arange(tile_total, dtype=jnp.int32), chosen_all, paired_all, keep_all))
    live = (block_rows.reshape(tile_total, CAP) >= 0)[:, :, None, None]
    purified = jnp.where(live, 3.0 * squares - 2.0 * cubes, 0.0)
    return purified.reshape(N_ROW, N_COL, CAP, BLK, BLK).astype(jnp.float32)
```

```python
import functools

import jax
import jax.numpy as jnp
from jax import lax
from jax.experimental import pallas as pl
from jax.experimental.pallas import tpu as pltpu
from jax.sharding import PartitionSpec as P

NEIGH = 7
CAP = 10
BLK = 64
PAIRS = CAP // 2
LANES = 128
SHIFT = 11
BIG = 1 << 30
MESH = pl.DeviceIdType.MESH


def own_keys(rows, cols):
    key = jnp.where(rows >= 0, (rows << SHIFT) | cols, -1)
    slot = lax.broadcasted_iota(jnp.int32, (16, CAP), 0)
    lane = lax.broadcasted_iota(jnp.int32, (16, CAP), 1)
    column = jnp.sum(jnp.where(slot == lane, key + 1, 0), axis=1, keepdims=True) - 1
    slot = lax.broadcasted_iota(jnp.int32, (16, LANES), 0)
    lane = lax.broadcasted_iota(jnp.int32, (16, LANES), 1)
    row = jnp.sum(jnp.where(lax.rem(lane, 16) == slot, column, 0), axis=0, keepdims=True)
    return column, row


def lane_dense(meta, tiles):
    lane = lax.broadcasted_iota(jnp.int32, (1, LANES), 1) // 16
    groups = []
    for base in range(0, tiles, 8):
        group = jnp.full((1, LANES), -1, jnp.int32)
        for m in range(min(8, tiles - base)):
            group = jnp.where(lane == m, meta[base + m], group)
        groups.append(group)
    return groups


def slot_ids(groups):
    lane = lax.broadcasted_iota(jnp.int32, (1, LANES), 1)
    return [(lane // 16 + 8 * g) * CAP + lax.rem(lane, 16) for g in range(groups)]


def pair_up(mine, left, right):
    ids_left, ids_right = slot_ids(len(left)), slot_ids(len(right))
    codes = []
    for keys, ids in zip(left, ids_left):
        same = ((keys >> SHIFT) == (mine >> SHIFT)) & (keys >= 0) & (mine >= 0)
        codes.append(jnp.where(same, (ids << SHIFT) | (keys & ((1 << SHIFT) - 1)), BIG))
    column = mine & ((1 << SHIFT) - 1)
    lane = lax.broadcasted_iota(jnp.int32, (16, LANES), 1)
    chosen = jnp.full((16, LANES), -1, jnp.int32)
    paired = jnp.full((16, LANES), -1, jnp.int32)
    for n in range(NEIGH):
        least = functools.reduce(jnp.minimum, codes)
        least = jnp.min(least, axis=1, keepdims=True)
        codes = [jnp.where(code == least, BIG, code) for code in codes]
        want = ((least & ((1 << SHIFT) - 1)) << SHIFT) | column
        hits = [jnp.where(keys == want, ids, -1) for keys, ids in zip(right, ids_right)]
        partner = jnp.max(functools.reduce(jnp.maximum, hits), axis=1, keepdims=True)
        good = (least < BIG) & (partner >= 0)
        chosen = jnp.where(lane == n, jnp.where(good, least >> SHIFT, -1), chosen)
        paired = jnp.where(lane == n, jnp.where(good, partner, -1), paired)
    return chosen, paired


def swap_halves(block):
    return jnp.concatenate([block[:, BLK:], block[:, :BLK]], axis=1)


def in_half(panel, code, half):
    block = panel[jnp.maximum(code, 0) >> 1]
    return jnp.where((code & 1) == half, block, swap_halves(block))


def left_row(panel, codes, out):
    low = lax.broadcasted_iota(jnp.int32, (BLK, LANES), 1) < BLK
    chunks = []
    for n in range(0, NEIGH + 1, 2):
        halves = []
        for half in range(2):
            if n + half < NEIGH:
                code = codes[out, n + half]
                block = in_half(panel, code, half)
                halves.append(jnp.where(code >= 0, block, jnp.zeros_like(block)))
            else:
                halves.append(jnp.zeros((BLK, LANES), panel.dtype))
        chunks.append(jnp.where(low, halves[0], halves[1]))
    return jnp.concatenate(chunks, axis=1)


def right_column(panel, codes, out):
    blocks = [in_half(panel, codes[16 + out, n], 0) for n in range(NEIGH)]
    return jnp.concatenate(blocks + [blocks[-1]], axis=0)


def kernel(
    nx, ny, nz,
    values, rows, cols, out,
    left_panel, right_panel, square_panel, stacked, square,
    left_meta, right_meta, codes_vector, codes,
    left_send, left_recv, square_send, square_recv,
    plane_send, plane_recv, twin_send, twin_recv,
    meta_send, meta_recv, codes_sem,
):
    plane = nx * ny
    me, z = lax.axis_index("row"), lax.axis_index("col")
    core = lax.rem(me, 2)
    x, y = me // (2 * ny), lax.rem(me // 2, ny)
    above, below = lax.rem(z + 1, nz), lax.rem(z + nz - 1, nz)
    twin = (me + 1 - 2 * core, z)

    def at_plane(dx, dy):
        return (lax.rem(x + dx + nx, nx) * ny + lax.rem(y + dy + ny, ny)) * 2 + core, z

    def at_depth(dz):
        return me, lax.rem(z + dz + nz, nz)

    z_steps = [1 << k for k in range(nz.bit_length() - 1)]
    y_steps = [1 << k for k in range(ny.bit_length() - 1)]
    x_steps = [1 << k for k in range(nx.bit_length() - 1)]

    barrier = pltpu.get_barrier_semaphore()
    greeted = [at_depth(1), twin] + [at_depth(-s) for s in z_steps]
    greeted += [at_plane(-(d // ny), -(d % ny)) for d in range(1, plane)]
    for device in greeted:
        pl.semaphore_signal(barrier, inc=1, device_id=device, device_id_type=MESH)

    mine, key_row = own_keys(rows[...], cols[...])
    left_meta[0] = key_row
    right_meta[0] = key_row
    for t in range(PAIRS):
        pair = jnp.concatenate([values[2 * t], values[2 * t + 1]], axis=1)
        left_panel[t] = pair
        right_panel[t] = pair
    pl.semaphore_wait(barrier, len(greeted))

    def hop(panel, send, recv, way, d, p):
        if way == 0:
            source, target, device = d - 1, d, above
        else:
            source, target, device = lax.rem(nz + 1 - d, nz), nz - d, below
        return pltpu.make_async_remote_copy(
            src_ref=panel.at[pl.ds(source * PAIRS + p, 1)],
            dst_ref=panel.at[pl.ds(target * PAIRS + p, 1)],
            send_sem=send.at[way, d - 1, p],
            recv_sem=recv.at[way, d - 1, p],
            device_id=(me, device),
            device_id_type=MESH,
        )

    far = nz // 2
    split = (PAIRS + 1) // 2

    def last_way(p):
        return 0 if p < split else 1

    def advance(panel, send, recv, d):
        for p in range(PAIRS):
            for way in range(2):
                hop(panel, send, recv, way, d, p).wait_recv()
                hop(panel, send, recv, way, d + 1, p).start()

    def finish(panel, send, recv):
        for p in range(PAIRS):
            for way in range(2):
                hop(panel, send, recv, way, far - 1, p).wait_recv()
                if last_way(p) == way:
                    hop(panel, send, recv, way, far, p).start()
        for p in range(PAIRS):
            hop(panel, send, recv, last_way(p), far, p).wait_recv()

    def settle(panel, send, recv):
        @pl.loop(1, far)
        def _(d):
            for p in range(PAIRS):
                for way in range(2):
                    hop(panel, send, recv, way, d, p).wait_send()

        for p in range(PAIRS):
            hop(panel, send, recv, last_way(p), far, p).wait_send()

    meta_copies = []
    for step in z_steps:
        meta_copies.append((left_meta, step, at_depth(step)))
    for step in y_steps:
        meta_copies.append((right_meta, step, at_plane(0, step)))
    for step in x_steps:
        meta_copies.append((right_meta, step * ny, at_plane(step, 0)))
    meta_copies.append((right_meta, plane, twin))
    meta_copies = [
        pltpu.make_async_remote_copy(
            src_ref=meta.at[pl.ds(0, count)],
            dst_ref=meta.at[pl.ds(count, count)],
            send_sem=meta_send.at[i],
            recv_sem=meta_recv.at[i],
            device_id=device,
            device_id_type=MESH,
        )
        for i, (meta, count, device) in enumerate(meta_copies)
    ]
    meta_left, meta_right = meta_copies[: len(z_steps)], meta_copies[len(z_steps) :]

    def to_plane(d):
        return pltpu.make_async_remote_copy(
            src_ref=right_panel.at[pl.ds(0, PAIRS)],
            dst_ref=right_panel.at[pl.ds(d * PAIRS, PAIRS)],
            send_sem=plane_send.at[d],
            recv_sem=plane_recv.at[d],
            device_id=at_plane(d // ny, lax.rem(d, ny)),
            device_id_type=MESH,
        )

    def to_twin(d):
        return pltpu.make_async_remote_copy(
            src_ref=right_panel.at[pl.ds(d * PAIRS, PAIRS)],
            dst_ref=right_panel.at[pl.ds((plane + d) * PAIRS, PAIRS)],
            send_sem=twin_send.at[d],
            recv_sem=twin_recv.at[d],
            device_id=twin,
            device_id_type=MESH,
        )

    left = (left_panel, left_send, left_recv)
    for p in range(PAIRS):
        for way in range(2):
            hop(*left, way, 1, p).start()
    meta_left[0].start()
    meta_right[0].start()
    to_twin(0).start()

    meta_rounds = max(len(meta_left), len(meta_right))
    for d in range(1, meta_rounds + 1):
        if d < far - 1:
            advance(*left, d)
        for chain in (meta_left, meta_right):
            if d <= len(chain):
                chain[d - 1].wait_recv()
                if d < len(chain):
                    chain[d].start()
        if d < plane:
            to_plane(d).start()
        if 2 < d < plane + 2:
            to_plane(d - 2).wait_recv()
            to_twin(d - 2).start()

    chosen, paired = pair_up(mine, lane_dense(left_meta, nz), lane_dense(right_meta, 2 * plane))
    codes_vector[0:16] = chosen
    codes_vector[16:32] = paired
    codes_copy = pltpu.make_async_copy(codes_vector, codes, codes_sem)
    codes_copy.start()

    next_d = meta_rounds + 1
    both = min(far - 1, plane)
    if next_d < both:
        @pl.loop(next_d, both)
        def _(d):
            advance(*left, d)
            to_plane(d).start()
            to_plane(d - 2).wait_recv()
            to_twin(d - 2).start()

    if max(next_d, both) < far - 1:
        @pl.loop(max(next_d, both), far - 1)
        def _(d):
            advance(*left, d)

    for d in range(max(next_d, both), plane + 2):
        if d < plane:
            to_plane(d).start()
        if 0 < d - 2 < plane:
            to_plane(d - 2).wait_recv()
            to_twin(d - 2).start()

    codes_copy.wait()
    finish(*left)

    @pl.loop(0, plane)
    def _(d):
        to_twin(d).wait_recv()

    second = (square_panel, square_send, square_recv)
    low = lax.broadcasted_iota(jnp.int32, (BLK, LANES), 1) < BLK
    for t in range(PAIRS):
        halves = []
        for half in range(2):
            o = 2 * t + half
            right = right_column(right_panel, codes, o)
            stacked[o] = right
            product = jnp.dot(left_row(left_panel, codes, o), right, preferred_element_type=jnp.float32)
            square[o] = product
            halves.append(product)
        pair = jnp.where(low, halves[0], swap_halves(halves[1]))
        square_panel[t] = pair.astype(square_panel.dtype)
        for way in range(2):
            hop(*second, way, 1, t).start()

    @pl.loop(1, far - 1)
    def _(d):
        advance(*second, d)

    finish(*second)

    for o in range(CAP):
        cube = jnp.dot(left_row(square_panel, codes, o), stacked[o], preferred_element_type=jnp.float32)
        out[o] = (3.0 * square[o] - 2.0 * cube)[:, :BLK]

    settle(*left)
    settle(*second)
    for copy in meta_copies:
        copy.wait_send()

    to_twin(0).wait_send()

    if plane > 1:
        @pl.loop(1, plane)
        def _(d):
            to_plane(d).wait_send()
            to_twin(d).wait_send()


def shards(nx, ny, nz, values, block_rows, block_cols):
    plane = nx * ny
    far = nz // 2
    metas = 2 * 16
    purified = pl.pallas_call(
        functools.partial(kernel, nx, ny, nz),
        out_shape=jax.ShapeDtypeStruct((CAP, BLK, BLK), jnp.float32),
        in_specs=[pl.BlockSpec(memory_space=pltpu.VMEM)] * 3,
        out_specs=pl.BlockSpec(memory_space=pltpu.VMEM),
        scratch_shapes=[
            pltpu.VMEM((nz * PAIRS, BLK, LANES), jnp.bfloat16),
            pltpu.VMEM((2 * plane * PAIRS, BLK, LANES), jnp.bfloat16),
            pltpu.VMEM((nz * PAIRS, BLK, LANES), jnp.bfloat16),
            pltpu.VMEM((CAP, 8 * BLK, LANES), jnp.bfloat16),
            pltpu.VMEM((CAP, BLK, LANES), jnp.float32),
            pltpu.VMEM((nz, 1, LANES), jnp.int32),
            pltpu.VMEM((2 * plane, 1, LANES), jnp.int32),
            pltpu.VMEM((32, LANES), jnp.int32),
            pltpu.SMEM((32, LANES), jnp.int32),
            pltpu.SemaphoreType.DMA((2, far, PAIRS)),
            pltpu.SemaphoreType.DMA((2, far, PAIRS)),
            pltpu.SemaphoreType.DMA((2, far, PAIRS)),
            pltpu.SemaphoreType.DMA((2, far, PAIRS)),
            pltpu.SemaphoreType.DMA((plane,)),
            pltpu.SemaphoreType.DMA((plane,)),
            pltpu.SemaphoreType.DMA((plane,)),
            pltpu.SemaphoreType.DMA((plane,)),
            pltpu.SemaphoreType.DMA((metas,)),
            pltpu.SemaphoreType.DMA((metas,)),
            pltpu.SemaphoreType.DMA,
        ],
        compiler_params=pltpu.CompilerParams(
            collective_id=0, has_side_effects=True, vmem_limit_bytes=40 * 1024 * 1024
        ),
    )(values.reshape(values.shape[2:]), block_rows.reshape(1, CAP), block_cols.reshape(1, CAP))
    return purified.reshape(values.shape)


PLANES = {32: (4, 4), 8: (2, 2), 2: (1, 1)}


def solution(mesh):
    nx, ny = PLANES[mesh.shape["row"]]
    body = functools.partial(shards, nx, ny, mesh.shape["col"])
    in_specs = (P("row", "col", None, None, None), P("row", "col", None), P("row", "col", None))
    out_specs = P("row", "col", None, None, None)
    return jax.shard_map(body, mesh=mesh, in_specs=in_specs, out_specs=out_specs, check_vma=False)
```

```python
import functools

import jax
import jax.numpy as jnp
from jax import lax
from jax.experimental import pallas as pl
from jax.experimental.pallas import tpu as pltpu
from jax.sharding import PartitionSpec as P

NEIGH = 7
CAP = 10
BLK = 64
PAIRS = CAP // 2
PIECES = ((0, 3), (3, 2))
LANES = 128
SHIFT = 11
BIG = 1 << 30
MESH = pl.DeviceIdType.MESH


def own_keys(rows, cols):
    key = jnp.where(rows >= 0, (rows << SHIFT) | cols, -1)
    slot = lax.broadcasted_iota(jnp.int32, (16, CAP), 0)
    lane = lax.broadcasted_iota(jnp.int32, (16, CAP), 1)
    column = jnp.sum(jnp.where(slot == lane, key + 1, 0), axis=1, keepdims=True) - 1
    slot = lax.broadcasted_iota(jnp.int32, (16, LANES), 0)
    lane = lax.broadcasted_iota(jnp.int32, (16, LANES), 1)
    row = jnp.sum(jnp.where(lax.rem(lane, 16) == slot, column, 0), axis=0, keepdims=True)
    return column, row


def lane_dense(meta, tiles):
    lane = lax.broadcasted_iota(jnp.int32, (1, LANES), 1) // 16
    groups = []
    for base in range(0, tiles, 8):
        group = jnp.full((1, LANES), -1, jnp.int32)
        for m in range(min(8, tiles - base)):
            group = jnp.where(lane == m, meta[base + m], group)
        groups.append(group)
    return groups


def slot_ids(groups):
    lane = lax.broadcasted_iota(jnp.int32, (1, LANES), 1)
    return [(lane // 16 + 8 * g) * CAP + lax.rem(lane, 16) for g in range(groups)]


def pair_up(mine, left, right):
    ids_left, ids_right = slot_ids(len(left)), slot_ids(len(right))
    codes = []
    for keys, ids in zip(left, ids_left):
        same = ((keys >> SHIFT) == (mine >> SHIFT)) & (keys >= 0) & (mine >= 0)
        codes.append(jnp.where(same, (ids << SHIFT) | (keys & ((1 << SHIFT) - 1)), BIG))
    column = mine & ((1 << SHIFT) - 1)
    lane = lax.broadcasted_iota(jnp.int32, (16, LANES), 1)
    chosen = jnp.full((16, LANES), -1, jnp.int32)
    paired = jnp.full((16, LANES), -1, jnp.int32)
    for n in range(NEIGH):
        least = functools.reduce(jnp.minimum, codes)
        least = jnp.min(least, axis=1, keepdims=True)
        codes = [jnp.where(code == least, BIG, code) for code in codes]
        want = ((least & ((1 << SHIFT) - 1)) << SHIFT) | column
        hits = [jnp.where(keys == want, ids, -1) for keys, ids in zip(right, ids_right)]
        partner = jnp.max(functools.reduce(jnp.maximum, hits), axis=1, keepdims=True)
        good = (least < BIG) & (partner >= 0)
        chosen = jnp.where(lane == n, jnp.where(good, least >> SHIFT, -1), chosen)
        paired = jnp.where(lane == n, jnp.where(good, partner, -1), paired)
    return chosen, paired


def swap_halves(block):
    return jnp.concatenate([block[:, BLK:], block[:, :BLK]], axis=1)


def in_half(panel, code, half):
    block = panel[jnp.maximum(code, 0) >> 1]
    return jnp.where((code & 1) == half, block, swap_halves(block))


def left_row(panel, codes, out):
    low = lax.broadcasted_iota(jnp.int32, (BLK, LANES), 1) < BLK
    chunks = []
    for n in range(0, NEIGH + 1, 2):
        halves = []
        for half in range(2):
            if n + half < NEIGH:
                code = codes[out, n + half]
                block = in_half(panel, code, half)
                halves.append(jnp.where(code >= 0, block, jnp.zeros_like(block)))
            else:
                halves.append(jnp.zeros((BLK, LANES), panel.dtype))
        chunks.append(jnp.where(low, halves[0], halves[1]))
    return jnp.concatenate(chunks, axis=1)


def right_column(panel, codes, out):
    blocks = [in_half(panel, codes[16 + out, n], 0) for n in range(NEIGH)]
    return jnp.concatenate(blocks + [blocks[-1]], axis=0)


def kernel(
    nx, ny, nz,
    values, rows, cols, out,
    left_panel, right_panel, square_panel, stacked, square,
    left_meta, right_meta, codes_vector, codes,
    left_send, left_recv, square_send, square_recv,
    plane_send, plane_recv, twin_send, twin_recv,
    meta_send, meta_recv, codes_sem,
):
    plane = nx * ny
    me, z = lax.axis_index("row"), lax.axis_index("col")
    core = lax.rem(me, 2)
    x, y = me // (2 * ny), lax.rem(me // 2, ny)
    twin = (me + 1 - 2 * core, z)

    def at_plane(dx, dy):
        return (lax.rem(x + dx + nx, nx) * ny + lax.rem(y + dy + ny, ny)) * 2 + core, z

    def at_depth(dz):
        return me, lax.rem(z + dz + nz, nz)

    z_steps = [1 << k for k in range(nz.bit_length() - 1)]
    y_steps = [1 << k for k in range(ny.bit_length() - 1)]
    x_steps = [1 << k for k in range(nx.bit_length() - 1)]

    barrier = pltpu.get_barrier_semaphore()
    greeted = [at_depth(1), at_depth(2), twin] + [at_depth(-s) for s in z_steps]
    greeted += [at_plane(-(d // ny), -(d % ny)) for d in range(1, plane)]
    for device in greeted:
        pl.semaphore_signal(barrier, inc=1, device_id=device, device_id_type=MESH)

    mine, key_row = own_keys(rows[...], cols[...])
    left_meta[0] = key_row
    right_meta[0] = key_row
    for t in range(PAIRS):
        pair = jnp.concatenate([values[2 * t], values[2 * t + 1]], axis=1)
        left_panel[t] = pair
        right_panel[t] = pair
    pl.semaphore_wait(barrier, len(greeted))

    far = nz // 2
    stages = far // 2

    def hop(ring, way, source, target, p):
        panel, send, recv = ring
        first, count = PIECES[p]
        gap = target - source
        if way == 0:
            here, there = source, target
        else:
            here, there, gap = lax.rem(nz - source, nz), nz - target, -gap
        return pltpu.make_async_remote_copy(
            src_ref=panel.at[pl.ds(here * PAIRS + first, count)],
            dst_ref=panel.at[pl.ds(there * PAIRS + first, count)],
            send_sem=send.at[way, target - 1, p],
            recv_sem=recv.at[way, target - 1, p],
            device_id=at_depth(gap),
            device_id_type=MESH,
        )

    lanes_of = [(p, way) for p in range(len(PIECES)) for way in range(2)]

    def stage(ring, k, p, way, wait=True, last=False):
        base = 2 * k - 2
        if wait:
            hop(ring, way, base - 2, base, p).wait_recv()
        if not last or way == p % 2:
            hop(ring, way, base, base + 2, p).start()
        hop(ring, way, base, base + 1, p).start()

    def arrive(ring):
        @pl.loop(1, stages + 1)
        def _(k):
            for p, way in lanes_of:
                hop(ring, way, 2 * k - 2, 2 * k - 1, p).wait_recv()

        for p in range(len(PIECES)):
            hop(ring, p % 2, far - 2, far, p).wait_recv()

    def settle(ring):
        @pl.loop(1, stages + 1)
        def _(k):
            for p, way in lanes_of:
                hop(ring, way, 2 * k - 2, 2 * k - 1, p).wait_send()

        @pl.loop(1, stages)
        def _(k):
            for p, way in lanes_of:
                hop(ring, way, 2 * k - 2, 2 * k, p).wait_send()

        for p in range(len(PIECES)):
            hop(ring, p % 2, far - 2, far, p).wait_send()

    metas = [(left_meta, step, at_depth(step)) for step in z_steps]
    metas += [(right_meta, step, at_plane(0, step)) for step in y_steps]
    metas += [(right_meta, step * ny, at_plane(step, 0)) for step in x_steps]
    metas += [(right_meta, plane, twin)]
    metas = [
        pltpu.make_async_remote_copy(
            src_ref=meta.at[pl.ds(0, count)],
            dst_ref=meta.at[pl.ds(count, count)],
            send_sem=meta_send.at[i],
            recv_sem=meta_recv.at[i],
            device_id=device,
            device_id_type=MESH,
        )
        for i, (meta, count, device) in enumerate(metas)
    ]
    chains = [metas[: len(z_steps)], metas[len(z_steps) :]]
    rounds = max(len(chain) for chain in chains)

    def to_plane(d):
        return pltpu.make_async_remote_copy(
            src_ref=right_panel.at[pl.ds(0, PAIRS)],
            dst_ref=right_panel.at[pl.ds(d * PAIRS, PAIRS)],
            send_sem=plane_send.at[d],
            recv_sem=plane_recv.at[d],
            device_id=at_plane(d // ny, lax.rem(d, ny)),
            device_id_type=MESH,
        )

    def to_twin(d):
        return pltpu.make_async_remote_copy(
            src_ref=right_panel.at[pl.ds(d * PAIRS, PAIRS)],
            dst_ref=right_panel.at[pl.ds((plane + d) * PAIRS, PAIRS)],
            send_sem=twin_send.at[d],
            recv_sem=twin_recv.at[d],
            device_id=twin,
            device_id_type=MESH,
        )

    group = -(-(plane - 1) // rounds)

    def beside(k):
        for chain in chains:
            if 0 < k <= len(chain):
                chain[k - 1].wait_recv()
            if k < len(chain):
                chain[k].start()
        if k == 0:
            to_twin(0).start()
        for d in range(1 + (k - 1) * group, min(plane, 1 + k * group)):
            if d > 0:
                to_plane(d).wait_recv()
                to_twin(d).start()
        for d in range(1 + k * group, min(plane, 1 + (k + 1) * group)):
            to_plane(d).start()
        if k == rounds:
            chosen, paired = pair_up(mine, lane_dense(left_meta, nz), lane_dense(right_meta, 2 * plane))
            codes_vector[0:16] = chosen
            codes_vector[16:32] = paired
            codes_copy.start()
        if k == rounds + 2:
            codes_copy.wait()

            @pl.loop(0, plane)
            def _(d):
                to_twin(d).wait_recv()

            @pl.loop(0, CAP)
            def _(o):
                stacked[o] = right_column(right_panel, codes, o)

    codes_copy = pltpu.make_async_copy(codes_vector, codes, codes_sem)
    first = (left_panel, left_send, left_recv)
    for k in range(max(stages, rounds + 3)):
        if k < stages:
            for p, way in lanes_of:
                stage(first, k + 1, p, way, wait=k > 0, last=k == stages - 1)
        beside(k)
    arrive(first)

    second = (square_panel, square_send, square_recv)
    low = lax.broadcasted_iota(jnp.int32, (BLK, LANES), 1) < BLK

    def square_pair(t):
        halves = []
        for half in range(2):
            o = 2 * t + half
            product = jnp.dot(left_row(left_panel, codes, o), stacked[o], preferred_element_type=jnp.float32)
            square[o] = product
            halves.append(product)
        pair = jnp.where(low, halves[0], swap_halves(halves[1]))
        square_panel[t] = pair.astype(square_panel.dtype)

    for p, (start, count) in enumerate(PIECES):
        pl.loop(start, start + count)(square_pair)
        for way in range(2):
            stage(second, 1, p, way, wait=False, last=stages == 1)

    if stages > 2:
        @pl.loop(2, stages)
        def _(k):
            for p, way in lanes_of:
                stage(second, k, p, way)

    if stages > 1:
        for p, way in lanes_of:
            stage(second, stages, p, way, last=True)
    arrive(second)

    @pl.loop(0, CAP)
    def _(o):
        cube = jnp.dot(left_row(square_panel, codes, o), stacked[o], preferred_element_type=jnp.float32)
        out[o] = (3.0 * square[o] - 2.0 * cube)[:, :BLK]

    settle(first)
    settle(second)
    for copy in metas:
        copy.wait_send()

    to_twin(0).wait_send()

    if plane > 1:
        @pl.loop(1, plane)
        def _(d):
            to_plane(d).wait_send()
            to_twin(d).wait_send()


def shards(nx, ny, nz, values, block_rows, block_cols):
    plane = nx * ny
    far = nz // 2
    metas = 2 * 16
    purified = pl.pallas_call(
        functools.partial(kernel, nx, ny, nz),
        out_shape=jax.ShapeDtypeStruct((CAP, BLK, BLK), jnp.float32),
        in_specs=[pl.BlockSpec(memory_space=pltpu.VMEM)] * 3,
        out_specs=pl.BlockSpec(memory_space=pltpu.VMEM),
        scratch_shapes=[
            pltpu.VMEM((nz * PAIRS, BLK, LANES), jnp.bfloat16),
            pltpu.VMEM((2 * plane * PAIRS, BLK, LANES), jnp.bfloat16),
            pltpu.VMEM((nz * PAIRS, BLK, LANES), jnp.bfloat16),
            pltpu.VMEM((CAP, 8 * BLK, LANES), jnp.bfloat16),
            pltpu.VMEM((CAP, BLK, LANES), jnp.float32),
            pltpu.VMEM((nz, 1, LANES), jnp.int32),
            pltpu.VMEM((2 * plane, 1, LANES), jnp.int32),
            pltpu.VMEM((32, LANES), jnp.int32),
            pltpu.SMEM((32, LANES), jnp.int32),
            pltpu.SemaphoreType.DMA((2, far, len(PIECES))),
            pltpu.SemaphoreType.DMA((2, far, len(PIECES))),
            pltpu.SemaphoreType.DMA((2, far, len(PIECES))),
            pltpu.SemaphoreType.DMA((2, far, len(PIECES))),
            pltpu.SemaphoreType.DMA((plane,)),
            pltpu.SemaphoreType.DMA((plane,)),
            pltpu.SemaphoreType.DMA((plane,)),
            pltpu.SemaphoreType.DMA((plane,)),
            pltpu.SemaphoreType.DMA((metas,)),
            pltpu.SemaphoreType.DMA((metas,)),
            pltpu.SemaphoreType.DMA,
        ],
        compiler_params=pltpu.CompilerParams(
            collective_id=0, has_side_effects=True, vmem_limit_bytes=40 * 1024 * 1024
        ),
    )(values.reshape(values.shape[2:]), block_rows.reshape(1, CAP), block_cols.reshape(1, CAP))
    return purified.reshape(values.shape)


PLANES = {32: (4, 4), 8: (2, 2), 2: (1, 1)}


def solution(mesh):
    nx, ny = PLANES[mesh.shape["row"]]
    body = functools.partial(shards, nx, ny, mesh.shape["col"])
    in_specs = (P("row", "col", None, None, None), P("row", "col", None), P("row", "col", None))
    out_specs = P("row", "col", None, None, None)
    return jax.shard_map(body, mesh=mesh, in_specs=in_specs, out_specs=out_specs, check_vma=False)
```

```python
import functools

import jax
import jax.numpy as jnp
from jax import lax
from jax.experimental import pallas as pl
from jax.experimental.pallas import tpu as pltpu
from jax.sharding import PartitionSpec as P

NEIGH = 7
CAP = 10
BLK = 64
PAIRS = CAP // 2
PIECES = ((0, 3), (3, 2))
KEYS = len(PIECES)
LANES = 128
SHIFT = 11
BIG = 1 << 30
MESH = pl.DeviceIdType.MESH


def own_keys(rows, cols):
    key = jnp.where(rows >= 0, (rows << SHIFT) | cols, -1)
    slot = lax.broadcasted_iota(jnp.int32, (16, CAP), 0)
    lane = lax.broadcasted_iota(jnp.int32, (16, CAP), 1)
    column = jnp.sum(jnp.where(slot == lane, key + 1, 0), axis=1, keepdims=True) - 1
    slot = lax.broadcasted_iota(jnp.int32, (16, LANES), 0)
    lane = lax.broadcasted_iota(jnp.int32, (16, LANES), 1)
    row = jnp.sum(jnp.where(lax.rem(lane, 16) == slot, column, 0), axis=0, keepdims=True)
    return column, row


def lane_dense(meta, tiles):
    lane = lax.broadcasted_iota(jnp.int32, (1, LANES), 1) // 16
    groups = []
    for base in range(0, tiles, 8):
        group = jnp.full((1, LANES), -1, jnp.int32)
        for m in range(min(8, tiles - base)):
            group = jnp.where(lane == m, meta[base + m], group)
        groups.append(group)
    return groups


def slot_ids(groups):
    lane = lax.broadcasted_iota(jnp.int32, (1, LANES), 1)
    return [(lane // 16 + 8 * g) * CAP + lax.rem(lane, 16) for g in range(groups)]


def pair_up(mine, left, right):
    ids_left, ids_right = slot_ids(len(left)), slot_ids(len(right))
    codes = []
    for keys, ids in zip(left, ids_left):
        same = ((keys >> SHIFT) == (mine >> SHIFT)) & (keys >= 0) & (mine >= 0)
        codes.append(jnp.where(same, (ids << SHIFT) | (keys & ((1 << SHIFT) - 1)), BIG))
    column = mine & ((1 << SHIFT) - 1)
    lane = lax.broadcasted_iota(jnp.int32, (16, LANES), 1)
    chosen = jnp.full((16, LANES), -1, jnp.int32)
    paired = jnp.full((16, LANES), -1, jnp.int32)
    for n in range(NEIGH):
        least = functools.reduce(jnp.minimum, codes)
        least = jnp.min(least, axis=1, keepdims=True)
        codes = [jnp.where(code == least, BIG, code) for code in codes]
        want = ((least & ((1 << SHIFT) - 1)) << SHIFT) | column
        hits = [jnp.where(keys == want, ids, -1) for keys, ids in zip(right, ids_right)]
        partner = jnp.max(functools.reduce(jnp.maximum, hits), axis=1, keepdims=True)
        good = (least < BIG) & (partner >= 0)
        chosen = jnp.where(lane == n, jnp.where(good, least >> SHIFT, -1), chosen)
        paired = jnp.where(lane == n, jnp.where(good, partner, -1), paired)
    return chosen, paired


def swap_halves(block):
    return jnp.concatenate([block[:, BLK:], block[:, :BLK]], axis=1)


def in_half(panel, code, half):
    block = panel[jnp.maximum(code, 0) >> 1]
    return jnp.where((code & 1) == half, block, swap_halves(block))


def left_row(panel, codes, out):
    low = lax.broadcasted_iota(jnp.int32, (BLK, LANES), 1) < BLK
    chunks = []
    for n in range(0, NEIGH + 1, 2):
        halves = []
        for half in range(2):
            if n + half < NEIGH:
                code = codes[out, n + half]
                block = in_half(panel, code, half)
                halves.append(jnp.where(code >= 0, block, jnp.zeros_like(block)))
            else:
                halves.append(jnp.zeros((BLK, LANES), panel.dtype))
        chunks.append(jnp.where(low, halves[0], halves[1]))
    return jnp.concatenate(chunks, axis=1)


def right_column(panel, codes, out):
    blocks = [in_half(panel, codes[16 + out, n], 0) for n in range(NEIGH)]
    return jnp.concatenate(blocks + [blocks[-1]], axis=0)


def kernel(
    nx, ny, nz,
    values, rows, cols, out,
    left_panel, right_panel, square_panel, stacked, square,
    left_meta, right_meta, codes_vector, codes,
    left_send, left_recv, square_send, square_recv,
    plane_send, plane_recv, twin_send, twin_recv,
    meta_send, meta_recv, codes_sem,
):
    plane = nx * ny
    me, z = lax.axis_index("row"), lax.axis_index("col")
    core = lax.rem(me, 2)
    x, y = me // (2 * ny), lax.rem(me // 2, ny)
    twin = (me + 1 - 2 * core, z)

    def at_plane(dx, dy):
        return (lax.rem(x + dx + nx, nx) * ny + lax.rem(y + dy + ny, ny)) * 2 + core, z

    def at_depth(dz):
        return me, lax.rem(z + dz + nz, nz)

    y_steps = [1 << k for k in range(ny.bit_length() - 1)]
    x_steps = [1 << k for k in range(nx.bit_length() - 1)]

    barrier = pltpu.get_barrier_semaphore()
    greeted = [twin] + [at_depth(s) for s in (1, 2, -1, -2)]
    greeted += [at_plane(-(d // ny), -(d % ny)) for d in range(1, plane)]
    for device in greeted:
        pl.semaphore_signal(barrier, inc=1, device_id=device, device_id_type=MESH)

    mine, key_row = own_keys(rows[...], cols[...])
    left_meta[0] = key_row
    right_meta[0] = key_row
    for t in range(PAIRS):
        pair = jnp.concatenate([values[2 * t], values[2 * t + 1]], axis=1)
        left_panel[t] = pair
        right_panel[t] = pair
    pl.semaphore_wait(barrier, len(greeted))

    far = nz // 2
    stages = far // 2

    def hop(ring, way, source, target, p):
        panel, keys, send, recv = ring
        gap = target - source
        if way == 0:
            here, there = source, target
        else:
            here, there, gap = lax.rem(nz - source, nz), nz - target, -gap
        if p == KEYS:
            src, dst = keys.at[pl.ds(here, 1)], keys.at[pl.ds(there, 1)]
        else:
            first, count = PIECES[p]
            src, dst = panel.at[pl.ds(here * PAIRS + first, count)], panel.at[pl.ds(there * PAIRS + first, count)]
        return pltpu.make_async_remote_copy(
            src_ref=src,
            dst_ref=dst,
            send_sem=send.at[way, target - 1, p],
            recv_sem=recv.at[way, target - 1, p],
            device_id=at_depth(gap),
            device_id_type=MESH,
        )

    pieces = tuple(range(len(PIECES)))

    def last_way(p):
        return 1 if p == 1 else 0

    def stage(ring, k, p, way, wait=True, last=False):
        base = 2 * k - 2
        if wait:
            hop(ring, way, base - 2, base, p).wait_recv()
        if not last or way == last_way(p):
            hop(ring, way, base, base + 2, p).start()
        hop(ring, way, base, base + 1, p).start()

    def arrive(ring, parts):
        @pl.loop(1, stages + 1)
        def _(k):
            for p in parts:
                for way in range(2):
                    hop(ring, way, 2 * k - 2, 2 * k - 1, p).wait_recv()

        for p in parts:
            hop(ring, last_way(p), far - 2, far, p).wait_recv()

    def settle(ring, parts):
        @pl.loop(1, stages + 1)
        def _(k):
            for p in parts:
                for way in range(2):
                    hop(ring, way, 2 * k - 2, 2 * k - 1, p).wait_send()

        @pl.loop(1, stages)
        def _(k):
            for p in parts:
                for way in range(2):
                    hop(ring, way, 2 * k - 2, 2 * k, p).wait_send()

        for p in parts:
            hop(ring, last_way(p), far - 2, far, p).wait_send()

    metas = [(right_meta, step, at_plane(0, step)) for step in y_steps]
    metas += [(right_meta, step * ny, at_plane(step, 0)) for step in x_steps]
    metas += [(right_meta, plane, twin)]
    metas = [
        pltpu.make_async_remote_copy(
            src_ref=meta.at[pl.ds(0, count)],
            dst_ref=meta.at[pl.ds(count, count)],
            send_sem=meta_send.at[i],
            recv_sem=meta_recv.at[i],
            device_id=device,
            device_id_type=MESH,
        )
        for i, (meta, count, device) in enumerate(metas)
    ]
    rounds = len(metas)

    def to_plane(d):
        return pltpu.make_async_remote_copy(
            src_ref=right_panel.at[pl.ds(0, PAIRS)],
            dst_ref=right_panel.at[pl.ds(d * PAIRS, PAIRS)],
            send_sem=plane_send.at[d],
            recv_sem=plane_recv.at[d],
            device_id=at_plane(d // ny, lax.rem(d, ny)),
            device_id_type=MESH,
        )

    def to_twin(d):
        return pltpu.make_async_remote_copy(
            src_ref=right_panel.at[pl.ds(d * PAIRS, PAIRS)],
            dst_ref=right_panel.at[pl.ds((plane + d) * PAIRS, PAIRS)],
            send_sem=twin_send.at[d],
            recv_sem=twin_recv.at[d],
            device_id=twin,
            device_id_type=MESH,
        )

    group = -(-(plane - 1) // rounds)

    def beside(k):
        if 0 < k <= rounds:
            metas[k - 1].wait_recv()
        if k < rounds:
            metas[k].start()
        if k == 0:
            to_twin(0).start()
        for d in range(1 + (k - 1) * group, min(plane, 1 + k * group)):
            if d > 0:
                to_plane(d).wait_recv()
                to_twin(d).start()
        for d in range(1 + k * group, min(plane, 1 + (k + 1) * group)):
            to_plane(d).start()

    codes_copy = pltpu.make_async_copy(codes_vector, codes, codes_sem)
    first = (left_panel, left_meta, left_send, left_recv)
    for k in range(max(stages, rounds + 1)):
        if k < stages:
            for p in (KEYS,) + pieces:
                for way in range(2):
                    stage(first, k + 1, p, way, wait=k > 0, last=k == stages - 1)
        beside(k)

    arrive(first, (KEYS,))
    chosen, paired = pair_up(mine, lane_dense(left_meta, nz), lane_dense(right_meta, 2 * plane))
    codes_vector[0:16] = chosen
    codes_vector[16:32] = paired
    codes_copy.start()

    @pl.loop(0, plane)
    def _(d):
        to_twin(d).wait_recv()

    codes_copy.wait()

    @pl.loop(0, CAP)
    def _(o):
        stacked[o] = right_column(right_panel, codes, o)

    arrive(first, pieces)

    second = (square_panel, None, square_send, square_recv)
    low = lax.broadcasted_iota(jnp.int32, (BLK, LANES), 1) < BLK

    def square_pair(t):
        halves = []
        for half in range(2):
            o = 2 * t + half
            product = jnp.dot(left_row(left_panel, codes, o), stacked[o], preferred_element_type=jnp.float32)
            square[o] = product
            halves.append(product)
        pair = jnp.where(low, halves[0], swap_halves(halves[1]))
        square_panel[t] = pair.astype(square_panel.dtype)

    for p, (start, count) in enumerate(PIECES):
        pl.loop(start, start + count)(square_pair)
        for way in range(2):
            stage(second, 1, p, way, wait=False, last=stages == 1)

    if stages > 2:
        @pl.loop(2, stages)
        def _(k):
            for p in pieces:
                for way in range(2):
                    stage(second, k, p, way)

    if stages > 1:
        for p in pieces:
            for way in range(2):
                stage(second, stages, p, way, last=True)
    arrive(second, pieces)

    @pl.loop(0, CAP)
    def _(o):
        cube = jnp.dot(left_row(square_panel, codes, o), stacked[o], preferred_element_type=jnp.float32)
        out[o] = (3.0 * square[o] - 2.0 * cube)[:, :BLK]

    settle(first, (KEYS,) + pieces)
    settle(second, pieces)
    for copy in metas:
        copy.wait_send()

    to_twin(0).wait_send()

    if plane > 1:
        @pl.loop(1, plane)
        def _(d):
            to_plane(d).wait_send()
            to_twin(d).wait_send()


def shards(nx, ny, nz, values, block_rows, block_cols):
    plane = nx * ny
    far = nz // 2
    metas = 2 * 16
    purified = pl.pallas_call(
        functools.partial(kernel, nx, ny, nz),
        out_shape=jax.ShapeDtypeStruct((CAP, BLK, BLK), jnp.float32),
        in_specs=[pl.BlockSpec(memory_space=pltpu.VMEM)] * 3,
        out_specs=pl.BlockSpec(memory_space=pltpu.VMEM),
        scratch_shapes=[
            pltpu.VMEM((nz * PAIRS, BLK, LANES), jnp.bfloat16),
            pltpu.VMEM((2 * plane * PAIRS, BLK, LANES), jnp.bfloat16),
            pltpu.VMEM((nz * PAIRS, BLK, LANES), jnp.bfloat16),
            pltpu.VMEM((CAP, 8 * BLK, LANES), jnp.bfloat16),
            pltpu.VMEM((CAP, BLK, LANES), jnp.float32),
            pltpu.VMEM((nz, 1, LANES), jnp.int32),
            pltpu.VMEM((2 * plane, 1, LANES), jnp.int32),
            pltpu.VMEM((32, LANES), jnp.int32),
            pltpu.SMEM((32, LANES), jnp.int32),
            pltpu.SemaphoreType.DMA((2, far, len(PIECES) + 1)),
            pltpu.SemaphoreType.DMA((2, far, len(PIECES) + 1)),
            pltpu.SemaphoreType.DMA((2, far, len(PIECES))),
            pltpu.SemaphoreType.DMA((2, far, len(PIECES))),
            pltpu.SemaphoreType.DMA((plane,)),
            pltpu.SemaphoreType.DMA((plane,)),
            pltpu.SemaphoreType.DMA((plane,)),
            pltpu.SemaphoreType.DMA((plane,)),
            pltpu.SemaphoreType.DMA((metas,)),
            pltpu.SemaphoreType.DMA((metas,)),
            pltpu.SemaphoreType.DMA,
        ],
        compiler_params=pltpu.CompilerParams(
            collective_id=0, has_side_effects=True, vmem_limit_bytes=40 * 1024 * 1024
        ),
    )(values.reshape(values.shape[2:]), block_rows.reshape(1, CAP), block_cols.reshape(1, CAP))
    return purified.reshape(values.shape)


PLANES = {32: (4, 4), 8: (2, 2), 2: (1, 1)}


def solution(mesh):
    nx, ny = PLANES[mesh.shape["row"]]
    body = functools.partial(shards, nx, ny, mesh.shape["col"])
    in_specs = (P("row", "col", None, None, None), P("row", "col", None), P("row", "col", None))
    out_specs = P("row", "col", None, None, None)
    return jax.shard_map(body, mesh=mesh, in_specs=in_specs, out_specs=out_specs, check_vma=False)
```

```python
import functools

import jax
import jax.numpy as jnp
from jax import lax
from jax.experimental import pallas as pl
from jax.experimental.pallas import tpu as pltpu
from jax.sharding import PartitionSpec as P

NEIGH = 7
CAP = 10
BLK = 64
PAIRS = CAP // 2
PIECES = ((0, 3), (3, 2))
KEYS = len(PIECES)
LANES = 128
SHIFT = 11
BIG = 1 << 30
MESH = pl.DeviceIdType.MESH


def own_keys(rows, cols):
    key = jnp.where(rows >= 0, (rows << SHIFT) | cols, -1)
    slot = lax.broadcasted_iota(jnp.int32, (16, CAP), 0)
    lane = lax.broadcasted_iota(jnp.int32, (16, CAP), 1)
    column = jnp.sum(jnp.where(slot == lane, key + 1, 0), axis=1, keepdims=True) - 1
    slot = lax.broadcasted_iota(jnp.int32, (16, LANES), 0)
    lane = lax.broadcasted_iota(jnp.int32, (16, LANES), 1)
    row = jnp.sum(jnp.where(lax.rem(lane, 16) == slot, column, 0), axis=0, keepdims=True)
    return column, row


def lane_dense(meta, tiles):
    lane = lax.broadcasted_iota(jnp.int32, (1, LANES), 1) // 16
    groups = []
    for base in range(0, tiles, 8):
        group = jnp.full((1, LANES), -1, jnp.int32)
        for m in range(min(8, tiles - base)):
            group = jnp.where(lane == m, meta[base + m], group)
        groups.append(group)
    return groups


def slot_ids(groups):
    lane = lax.broadcasted_iota(jnp.int32, (1, LANES), 1)
    return [(lane // 16 + 8 * g) * CAP + lax.rem(lane, 16) for g in range(groups)]


def pair_up(mine, left, right):
    ids_left, ids_right = slot_ids(len(left)), slot_ids(len(right))
    codes = []
    for keys, ids in zip(left, ids_left):
        same = ((keys >> SHIFT) == (mine >> SHIFT)) & (keys >= 0) & (mine >= 0)
        codes.append(jnp.where(same, (ids << SHIFT) | (keys & ((1 << SHIFT) - 1)), BIG))
    column = mine & ((1 << SHIFT) - 1)
    lane = lax.broadcasted_iota(jnp.int32, (16, LANES), 1)
    chosen = jnp.full((16, LANES), -1, jnp.int32)
    paired = jnp.full((16, LANES), -1, jnp.int32)
    for n in range(NEIGH):
        least = functools.reduce(jnp.minimum, codes)
        least = jnp.min(least, axis=1, keepdims=True)
        codes = [jnp.where(code == least, BIG, code) for code in codes]
        want = ((least & ((1 << SHIFT) - 1)) << SHIFT) | column
        hits = [jnp.where(keys == want, ids, -1) for keys, ids in zip(right, ids_right)]
        partner = jnp.max(functools.reduce(jnp.maximum, hits), axis=1, keepdims=True)
        good = (least < BIG) & (partner >= 0)
        chosen = jnp.where(lane == n, jnp.where(good, least >> SHIFT, -1), chosen)
        paired = jnp.where(lane == n, jnp.where(good, partner, -1), paired)
    return chosen, paired


def swap_halves(block):
    return jnp.concatenate([block[:, BLK:], block[:, :BLK]], axis=1)


def in_half(panel, code, half):
    block = panel[jnp.maximum(code, 0) >> 1]
    return jnp.where((code & 1) == half, block, swap_halves(block))


def left_row(panel, codes, out):
    low = lax.broadcasted_iota(jnp.int32, (BLK, LANES), 1) < BLK
    chunks = []
    for n in range(0, NEIGH + 1, 2):
        halves = []
        for half in range(2):
            if n + half < NEIGH:
                code = codes[out, n + half]
                block = in_half(panel, code, half)
                halves.append(jnp.where(code >= 0, block, jnp.zeros_like(block)))
            else:
                halves.append(jnp.zeros((BLK, LANES), panel.dtype))
        chunks.append(jnp.where(low, halves[0], halves[1]))
    return jnp.concatenate(chunks, axis=1)


def right_column(panel, codes, out):
    blocks = [in_half(panel, codes[16 + out, n], 0) for n in range(NEIGH)]
    return jnp.concatenate(blocks + [blocks[-1]], axis=0)


def kernel(
    nx, ny, nz,
    values_hbm, rows_hbm, cols_hbm, out,
    values, rows, cols, in_sem,
    left_panel, right_panel, square_panel, stacked, square,
    left_meta, right_meta, codes_vector, codes,
    left_send, left_recv, square_send, square_recv,
    plane_send, plane_recv, twin_send, twin_recv,
    meta_send, meta_recv, codes_sem,
):
    plane = nx * ny
    me, z = lax.axis_index("row"), lax.axis_index("col")
    core = lax.rem(me, 2)
    x, y = me // (2 * ny), lax.rem(me // 2, ny)
    twin = (me + 1 - 2 * core, z)

    def at_plane(dx, dy):
        return (lax.rem(x + dx + nx, nx) * ny + lax.rem(y + dy + ny, ny)) * 2 + core, z

    def at_depth(dz):
        return me, lax.rem(z + dz + nz, nz)

    y_steps = [1 << k for k in range(ny.bit_length() - 1)]
    x_steps = [1 << k for k in range(nx.bit_length() - 1)]

    reads = [
        pltpu.make_async_copy(source, target, in_sem.at[i])
        for i, (source, target) in enumerate(((rows_hbm, rows), (cols_hbm, cols), (values_hbm, values)))
    ]
    for read in reads:
        read.start()

    barrier = pltpu.get_barrier_semaphore()
    greeted = [twin] + [at_depth(s) for s in (1, 2, -1, -2)]
    greeted += [at_plane(-(d // ny), -(d % ny)) for d in range(1, plane)]
    for device in greeted:
        pl.semaphore_signal(barrier, inc=1, device_id=device, device_id_type=MESH)

    for read in reads:
        read.wait()
    mine, key_row = own_keys(rows[...], cols[...])
    left_meta[0] = key_row
    right_meta[0] = key_row
    for t in range(PAIRS):
        pair = jnp.concatenate([values[2 * t], values[2 * t + 1]], axis=1)
        left_panel[t] = pair
        right_panel[t] = pair
    pl.semaphore_wait(barrier, len(greeted))

    far = nz // 2
    stages = far // 2
    depth = {gap: at_depth(gap) for gap in (1, 2, -1, -2)}

    def hop(ring, way, source, target, p):
        panel, keys, send, recv = ring
        gap = target - source
        if way == 0:
            here, there = source, target
        else:
            here, there, gap = (nz - source) % nz, nz - target, -gap
        if p == KEYS:
            src, dst = keys.at[pl.ds(here, 1)], keys.at[pl.ds(there, 1)]
        else:
            first, count = PIECES[p]
            src, dst = panel.at[pl.ds(here * PAIRS + first, count)], panel.at[pl.ds(there * PAIRS + first, count)]
        return pltpu.make_async_remote_copy(
            src_ref=src,
            dst_ref=dst,
            send_sem=send.at[way, target - 1, p],
            recv_sem=recv.at[way, target - 1, p],
            device_id=depth[gap],
            device_id_type=MESH,
        )

    pieces = tuple(range(len(PIECES)))

    def last_way(p):
        return 1 if p == 1 else 0

    def stage(ring, k, p, way):
        base, last = 2 * k - 2, k == stages
        if k > 1:
            hop(ring, way, base - 2, base, p).wait_recv()
        if not last or way == last_way(p):
            hop(ring, way, base, base + 2, p).start()
        hop(ring, way, base, base + 1, p).start()

    def between_in(ring, k, parts):
        for p in parts:
            for way in range(2):
                hop(ring, way, 2 * k - 2, 2 * k - 1, p).wait_recv()

    def sent(ring, k, parts):
        for p in parts:
            for way in range(2):
                hop(ring, way, 2 * k - 2, 2 * k - 1, p).wait_send()
                if k < stages or way == last_way(p):
                    hop(ring, way, 2 * k - 2, 2 * k, p).wait_send()

    def last_in(ring, parts):
        for p in parts:
            hop(ring, last_way(p), far - 2, far, p).wait_recv()
        between_in(ring, stages, parts)

    metas = [(right_meta, step, at_plane(0, step)) for step in y_steps]
    metas += [(right_meta, step * ny, at_plane(step, 0)) for step in x_steps]
    metas += [(right_meta, plane, twin)]
    metas = [
        pltpu.make_async_remote_copy(
            src_ref=meta.at[pl.ds(0, count)],
            dst_ref=meta.at[pl.ds(count, count)],
            send_sem=meta_send.at[i],
            recv_sem=meta_recv.at[i],
            device_id=device,
            device_id_type=MESH,
        )
        for i, (meta, count, device) in enumerate(metas)
    ]
    rounds = len(metas)

    def to_plane(d):
        return pltpu.make_async_remote_copy(
            src_ref=right_panel.at[pl.ds(0, PAIRS)],
            dst_ref=right_panel.at[pl.ds(d * PAIRS, PAIRS)],
            send_sem=plane_send.at[d],
            recv_sem=plane_recv.at[d],
            device_id=at_plane(d // ny, lax.rem(d, ny)),
            device_id_type=MESH,
        )

    def to_twin(d):
        return pltpu.make_async_remote_copy(
            src_ref=right_panel.at[pl.ds(d * PAIRS, PAIRS)],
            dst_ref=right_panel.at[pl.ds((plane + d) * PAIRS, PAIRS)],
            send_sem=twin_send.at[d],
            recv_sem=twin_recv.at[d],
            device_id=twin,
            device_id_type=MESH,
        )

    group = -(-(plane - 1) // rounds)

    def beside(k):
        if 0 < k <= rounds:
            metas[k - 1].wait_recv()
        if k < rounds:
            metas[k].start()
        if k == 0:
            to_twin(0).start()
        for d in range(1 + (k - 1) * group, min(plane, 1 + k * group)):
            if d > 0:
                to_plane(d).wait_recv()
                to_twin(d).start()
        for d in range(1 + k * group, min(plane, 1 + (k + 1) * group)):
            to_plane(d).start()

    codes_copy = pltpu.make_async_copy(codes_vector, codes, codes_sem)
    first = (left_panel, left_meta, left_send, left_recv)
    for k in range(max(stages, rounds + 1)):
        if k < stages:
            for p in (KEYS,) + pieces:
                for way in range(2):
                    stage(first, k + 1, p, way)
        beside(k)
        if 0 < k < stages:
            between_in(first, k, (KEYS,) + pieces)

    last_in(first, (KEYS,))
    chosen, paired = pair_up(mine, lane_dense(left_meta, nz), lane_dense(right_meta, 2 * plane))
    codes_vector[0:16] = chosen
    codes_vector[16:32] = paired
    codes_copy.start()

    @pl.loop(0, plane)
    def _(d):
        to_twin(d).wait_recv()

    codes_copy.wait()

    @pl.loop(0, CAP)
    def _(o):
        stacked[o] = right_column(right_panel, codes, o)

    last_in(first, pieces)

    second = (square_panel, None, square_send, square_recv)
    low = lax.broadcasted_iota(jnp.int32, (BLK, LANES), 1) < BLK

    def square_pair(t):
        halves = []
        for half in range(2):
            o = 2 * t + half
            product = jnp.dot(left_row(left_panel, codes, o), stacked[o], preferred_element_type=jnp.float32)
            square[o] = product
            halves.append(product)
        pair = jnp.where(low, halves[0], swap_halves(halves[1]))
        square_panel[t] = pair.astype(square_panel.dtype)

    for p, (start, count) in enumerate(PIECES):
        pl.loop(start, start + count)(square_pair)
        for way in range(2):
            stage(second, 1, p, way)

    for k in range(1, stages + 1):
        if k > 1:
            for p in pieces:
                for way in range(2):
                    stage(second, k, p, way)
            between_in(second, k - 1, pieces)
            sent(second, k - 1, pieces)
        sent(first, k, (KEYS,) + pieces)
        for copy in (metas + [to_twin(d) for d in range(plane)] + [to_plane(d) for d in range(1, plane)])[k - 1 :: stages]:
            copy.wait_send()
    last_in(second, pieces)

    @pl.loop(0, CAP)
    def _(o):
        cube = jnp.dot(left_row(square_panel, codes, o), stacked[o], preferred_element_type=jnp.float32)
        out[o] = (3.0 * square[o] - 2.0 * cube)[:, :BLK]

    sent(second, stages, pieces)


def shards(nx, ny, nz, values, block_rows, block_cols):
    plane = nx * ny
    far = nz // 2
    metas = 2 * 16
    purified = pl.pallas_call(
        functools.partial(kernel, nx, ny, nz),
        out_shape=jax.ShapeDtypeStruct((CAP, BLK, BLK), jnp.float32),
        in_specs=[pl.BlockSpec(memory_space=pl.ANY)] * 3,
        out_specs=pl.BlockSpec(memory_space=pltpu.VMEM),
        scratch_shapes=[
            pltpu.VMEM((CAP, BLK, BLK), jnp.bfloat16),
            pltpu.VMEM((1, CAP), jnp.int32),
            pltpu.VMEM((1, CAP), jnp.int32),
            pltpu.SemaphoreType.DMA((3,)),
            pltpu.VMEM((nz * PAIRS, BLK, LANES), jnp.bfloat16),
            pltpu.VMEM((2 * plane * PAIRS, BLK, LANES), jnp.bfloat16),
            pltpu.VMEM((nz * PAIRS, BLK, LANES), jnp.bfloat16),
            pltpu.VMEM((CAP, 8 * BLK, LANES), jnp.bfloat16),
            pltpu.VMEM((CAP, BLK, LANES), jnp.float32),
            pltpu.VMEM((nz, 1, LANES), jnp.int32),
            pltpu.VMEM((2 * plane, 1, LANES), jnp.int32),
            pltpu.VMEM((32, LANES), jnp.int32),
            pltpu.SMEM((32, LANES), jnp.int32),
            pltpu.SemaphoreType.DMA((2, far, len(PIECES) + 1)),
            pltpu.SemaphoreType.DMA((2, far, len(PIECES) + 1)),
            pltpu.SemaphoreType.DMA((2, far, len(PIECES))),
            pltpu.SemaphoreType.DMA((2, far, len(PIECES))),
            pltpu.SemaphoreType.DMA((plane,)),
            pltpu.SemaphoreType.DMA((plane,)),
            pltpu.SemaphoreType.DMA((plane,)),
            pltpu.SemaphoreType.DMA((plane,)),
            pltpu.SemaphoreType.DMA((metas,)),
            pltpu.SemaphoreType.DMA((metas,)),
            pltpu.SemaphoreType.DMA,
        ],
        compiler_params=pltpu.CompilerParams(
            collective_id=0, has_side_effects=True, vmem_limit_bytes=60 * 1024 * 1024
        ),
    )(values.reshape(values.shape[2:]), block_rows.reshape(1, CAP), block_cols.reshape(1, CAP))
    return purified.reshape(values.shape)


PLANES = {32: (4, 4), 8: (2, 2), 2: (1, 1)}


def solution(mesh):
    nx, ny = PLANES[mesh.shape["row"]]
    body = functools.partial(shards, nx, ny, mesh.shape["col"])
    in_specs = (P("row", "col", None, None, None), P("row", "col", None), P("row", "col", None))
    out_specs = P("row", "col", None, None, None)
    return jax.shard_map(body, mesh=mesh, in_specs=in_specs, out_specs=out_specs, check_vma=False)
```

```python
import functools

import jax
import jax.numpy as jnp
from jax import lax
from jax.experimental import pallas as pl
from jax.experimental.pallas import tpu as pltpu
from jax.sharding import PartitionSpec as P

NEIGH = 7
CAP = 10
BLK = 64
PAIRS = CAP // 2
PIECES = ((0, 3), (3, 2))
KEYS = len(PIECES)
LANES = 128
SHIFT = 11
BIG = 1 << 30
MESH = pl.DeviceIdType.MESH


def own_keys(rows, cols):
    key = jnp.where(rows >= 0, (rows << SHIFT) | cols, -1)
    slot = lax.broadcasted_iota(jnp.int32, (16, CAP), 0)
    lane = lax.broadcasted_iota(jnp.int32, (16, CAP), 1)
    column = jnp.sum(jnp.where(slot == lane, key + 1, 0), axis=1, keepdims=True) - 1
    slot = lax.broadcasted_iota(jnp.int32, (16, LANES), 0)
    lane = lax.broadcasted_iota(jnp.int32, (16, LANES), 1)
    row = jnp.sum(jnp.where(lax.rem(lane, 16) == slot, column, 0), axis=0, keepdims=True)
    return column, row


def lane_dense(meta, tiles):
    lane = lax.broadcasted_iota(jnp.int32, (1, LANES), 1) // 16
    groups = []
    for base in range(0, tiles, 8):
        group = jnp.full((1, LANES), -1, jnp.int32)
        for m in range(min(8, tiles - base)):
            group = jnp.where(lane == m, meta[base + m], group)
        groups.append(group)
    return groups


def slot_ids(groups):
    lane = lax.broadcasted_iota(jnp.int32, (1, LANES), 1)
    return [(lane // 16 + 8 * g) * CAP + lax.rem(lane, 16) for g in range(groups)]


def pair_up(mine, left, right):
    ids_left, ids_right = slot_ids(len(left)), slot_ids(len(right))
    codes = []
    for keys, ids in zip(left, ids_left):
        same = ((keys >> SHIFT) == (mine >> SHIFT)) & (keys >= 0) & (mine >= 0)
        codes.append(jnp.where(same, (ids << SHIFT) | (keys & ((1 << SHIFT) - 1)), BIG))
    column = mine & ((1 << SHIFT) - 1)
    lane = lax.broadcasted_iota(jnp.int32, (16, LANES), 1)
    chosen = jnp.full((16, LANES), -1, jnp.int32)
    paired = jnp.full((16, LANES), -1, jnp.int32)
    for n in range(NEIGH):
        least = functools.reduce(jnp.minimum, codes)
        least = jnp.min(least, axis=1, keepdims=True)
        codes = [jnp.where(code == least, BIG, code) for code in codes]
        want = ((least & ((1 << SHIFT) - 1)) << SHIFT) | column
        hits = [jnp.where(keys == want, ids, -1) for keys, ids in zip(right, ids_right)]
        partner = jnp.max(functools.reduce(jnp.maximum, hits), axis=1, keepdims=True)
        good = (least < BIG) & (partner >= 0)
        chosen = jnp.where(lane == n, jnp.where(good, least >> SHIFT, -1), chosen)
        paired = jnp.where(lane == n, jnp.where(good, partner, -1), paired)
    return chosen, paired


def swap_halves(block):
    return jnp.concatenate([block[:, BLK:], block[:, :BLK]], axis=1)


def in_half(panel, code, half):
    block = panel[jnp.maximum(code, 0) >> 1]
    return jnp.where((code & 1) == half, block, swap_halves(block))


def left_row(panel, codes, out):
    low = lax.broadcasted_iota(jnp.int32, (BLK, LANES), 1) < BLK
    chunks = []
    for n in range(0, NEIGH + 1, 2):
        halves = []
        for half in range(2):
            if n + half < NEIGH:
                code = codes[out, n + half]
                block = in_half(panel, code, half)
                halves.append(jnp.where(code >= 0, block, jnp.zeros_like(block)))
            else:
                halves.append(jnp.zeros((BLK, LANES), panel.dtype))
        chunks.append(jnp.where(low, halves[0], halves[1]))
    return jnp.concatenate(chunks, axis=1)


def right_column(panel, codes, out):
    blocks = [in_half(panel, codes[16 + out, n], 0) for n in range(NEIGH)]
    return jnp.concatenate(blocks + [blocks[-1]], axis=0)


def kernel(
    nx, ny, nz,
    values_hbm, rows_hbm, cols_hbm, out,
    values, rows, cols, in_sem,
    left_panel, right_panel, square_panel, stacked, square,
    left_meta, right_meta, codes_vector, codes,
    left_send, left_recv, square_send, square_recv,
    plane_send, plane_recv, twin_send, twin_recv,
    meta_send, meta_recv, codes_sem,
):
    plane = nx * ny
    me, z = lax.axis_index("row"), lax.axis_index("col")
    core = lax.rem(me, 2)
    x, y = me // (2 * ny), lax.rem(me // 2, ny)
    twin = (me + 1 - 2 * core, z)

    def at_plane(dx, dy):
        return (lax.rem(x + dx + nx, nx) * ny + lax.rem(y + dy + ny, ny)) * 2 + core, z

    def at_depth(dz):
        return me, lax.rem(z + dz + nz, nz)

    y_steps = [1 << k for k in range(ny.bit_length() - 1)]
    x_steps = [1 << k for k in range(nx.bit_length() - 1)]

    reads = [
        pltpu.make_async_copy(source, target, in_sem.at[i])
        for i, (source, target) in enumerate(((rows_hbm, rows), (cols_hbm, cols), (values_hbm, values)))
    ]
    for read in reads:
        read.start()

    barrier = pltpu.get_barrier_semaphore()
    greeted = [twin] + [at_depth(s) for s in (1, 2, -1, -2)]
    greeted += [at_plane(0, -d) for d in range(1, ny)] + [at_plane(-d, 0) for d in range(1, nx)]
    for device in greeted:
        pl.semaphore_signal(barrier, inc=1, device_id=device, device_id_type=MESH)

    for read in reads:
        read.wait()
    mine, key_row = own_keys(rows[...], cols[...])
    left_meta[0] = key_row
    right_meta[0] = key_row
    for t in range(PAIRS):
        pair = jnp.concatenate([values[2 * t], values[2 * t + 1]], axis=1)
        left_panel[t] = pair
        right_panel[t] = pair
    pl.semaphore_wait(barrier, len(greeted))

    far = nz // 2
    stages = far // 2
    depth = {gap: at_depth(gap) for gap in (1, 2, -1, -2)}

    def hop(ring, way, source, target, p):
        panel, keys, send, recv = ring
        gap = target - source
        if way == 0:
            here, there = source, target
        else:
            here, there, gap = (nz - source) % nz, nz - target, -gap
        if p == KEYS:
            src, dst = keys.at[pl.ds(here, 1)], keys.at[pl.ds(there, 1)]
        else:
            first, count = PIECES[p]
            src, dst = panel.at[pl.ds(here * PAIRS + first, count)], panel.at[pl.ds(there * PAIRS + first, count)]
        return pltpu.make_async_remote_copy(
            src_ref=src,
            dst_ref=dst,
            send_sem=send.at[way, target - 1, p],
            recv_sem=recv.at[way, target - 1, p],
            device_id=depth[gap],
            device_id_type=MESH,
        )

    pieces = tuple(range(len(PIECES)))

    def last_way(p):
        return 1 if p == 1 else 0

    def stage(ring, k, p, way):
        base, last = 2 * k - 2, k == stages
        if k > 1:
            hop(ring, way, base - 2, base, p).wait_recv()
        if not last or way == last_way(p):
            hop(ring, way, base, base + 2, p).start()
        hop(ring, way, base, base + 1, p).start()

    def between_in(ring, k, parts):
        for p in parts:
            for way in range(2):
                hop(ring, way, 2 * k - 2, 2 * k - 1, p).wait_recv()

    def sent(ring, k, parts):
        for p in parts:
            for way in range(2):
                hop(ring, way, 2 * k - 2, 2 * k - 1, p).wait_send()
                if k < stages or way == last_way(p):
                    hop(ring, way, 2 * k - 2, 2 * k, p).wait_send()

    def last_in(ring, parts):
        for p in parts:
            hop(ring, last_way(p), far - 2, far, p).wait_recv()
        between_in(ring, stages, parts)

    metas = [(right_meta, step, at_plane(0, step)) for step in y_steps]
    metas += [(right_meta, step * ny, at_plane(step, 0)) for step in x_steps]
    metas += [(right_meta, plane, twin)]
    metas = [
        pltpu.make_async_remote_copy(
            src_ref=meta.at[pl.ds(0, count)],
            dst_ref=meta.at[pl.ds(count, count)],
            send_sem=meta_send.at[i],
            recv_sem=meta_recv.at[i],
            device_id=device,
            device_id_type=MESH,
        )
        for i, (meta, count, device) in enumerate(metas)
    ]
    rounds = len(metas)

    def tiles_to(device, source, target, count, send_sem, recv_sem):
        return pltpu.make_async_remote_copy(
            src_ref=right_panel.at[pl.ds(source * PAIRS, count * PAIRS)],
            dst_ref=right_panel.at[pl.ds(target * PAIRS, count * PAIRS)],
            send_sem=send_sem,
            recv_sem=recv_sem,
            device_id=device,
            device_id_type=MESH,
        )

    along_y = [None] + [
        tiles_to(at_plane(0, d), 0, d, 1, plane_send.at[d], plane_recv.at[d]) for d in range(1, ny)
    ]
    along_x = [None] + [
        tiles_to(at_plane(d, 0), 0, d * ny, ny, plane_send.at[ny + d], plane_recv.at[ny + d]) for d in range(1, nx)
    ]
    to_twin = [
        tiles_to(twin, d * ny, plane + d * ny, ny, twin_send.at[d], twin_recv.at[d]) for d in range(nx)
    ]

    def beside(k):
        if 0 < k <= rounds:
            metas[k - 1].wait_recv()
        if k < rounds:
            metas[k].start()
        if k == 0:
            for copy in along_y[1:]:
                copy.start()
        if k == 1:
            for copy in along_y[1:]:
                copy.wait_recv()
            for copy in along_x[1:]:
                copy.start()
            to_twin[0].start()
        for d in range(1, nx):
            if k == (5 if d == 2 else 4):
                along_x[d].wait_recv()
                to_twin[d].start()

    codes_copy = pltpu.make_async_copy(codes_vector, codes, codes_sem)
    first = (left_panel, left_meta, left_send, left_recv)
    for k in range(max(stages, rounds + 1, 6)):
        if k < stages:
            for p in (KEYS,) + pieces:
                for way in range(2):
                    stage(first, k + 1, p, way)
        beside(k)
        if 0 < k < stages:
            between_in(first, k, (KEYS,) + pieces)

    last_in(first, (KEYS,))
    chosen, paired = pair_up(mine, lane_dense(left_meta, nz), lane_dense(right_meta, 2 * plane))
    codes_vector[0:16] = chosen
    codes_vector[16:32] = paired
    codes_copy.start()

    for copy in to_twin:
        copy.wait_recv()

    codes_copy.wait()

    @pl.loop(0, CAP)
    def _(o):
        stacked[o] = right_column(right_panel, codes, o)

    last_in(first, pieces)

    second = (square_panel, None, square_send, square_recv)
    low = lax.broadcasted_iota(jnp.int32, (BLK, LANES), 1) < BLK

    def square_pair(t):
        halves = []
        for half in range(2):
            o = 2 * t + half
            product = jnp.dot(left_row(left_panel, codes, o), stacked[o], preferred_element_type=jnp.float32)
            square[o] = product
            halves.append(product)
        pair = jnp.where(low, halves[0], swap_halves(halves[1]))
        square_panel[t] = pair.astype(square_panel.dtype)

    for p, (start, count) in enumerate(PIECES):
        pl.loop(start, start + count)(square_pair)
        for way in range(2):
            stage(second, 1, p, way)

    for k in range(1, stages + 1):
        if k > 1:
            for p in pieces:
                for way in range(2):
                    stage(second, k, p, way)
            between_in(second, k - 1, pieces)
            sent(second, k - 1, pieces)
        sent(first, k, (KEYS,) + pieces)
        for copy in (metas + to_twin + along_y[1:] + along_x[1:])[k - 1 :: stages]:
            copy.wait_send()
    last_in(second, pieces)

    @pl.loop(0, CAP)
    def _(o):
        cube = jnp.dot(left_row(square_panel, codes, o), stacked[o], preferred_element_type=jnp.float32)
        out[o] = (3.0 * square[o] - 2.0 * cube)[:, :BLK]

    sent(second, stages, pieces)


def shards(nx, ny, nz, values, block_rows, block_cols):
    plane = nx * ny
    far = nz // 2
    metas = 2 * 16
    purified = pl.pallas_call(
        functools.partial(kernel, nx, ny, nz),
        out_shape=jax.ShapeDtypeStruct((CAP, BLK, BLK), jnp.float32),
        in_specs=[pl.BlockSpec(memory_space=pl.ANY)] * 3,
        out_specs=pl.BlockSpec(memory_space=pltpu.VMEM),
        scratch_shapes=[
            pltpu.VMEM((CAP, BLK, BLK), jnp.bfloat16),
            pltpu.VMEM((1, CAP), jnp.int32),
            pltpu.VMEM((1, CAP), jnp.int32),
            pltpu.SemaphoreType.DMA((3,)),
            pltpu.VMEM((nz * PAIRS, BLK, LANES), jnp.bfloat16),
            pltpu.VMEM((2 * plane * PAIRS, BLK, LANES), jnp.bfloat16),
            pltpu.VMEM((nz * PAIRS, BLK, LANES), jnp.bfloat16),
            pltpu.VMEM((CAP, 8 * BLK, LANES), jnp.bfloat16),
            pltpu.VMEM((CAP, BLK, LANES), jnp.float32),
            pltpu.VMEM((nz, 1, LANES), jnp.int32),
            pltpu.VMEM((2 * plane, 1, LANES), jnp.int32),
            pltpu.VMEM((32, LANES), jnp.int32),
            pltpu.SMEM((32, LANES), jnp.int32),
            pltpu.SemaphoreType.DMA((2, far, len(PIECES) + 1)),
            pltpu.SemaphoreType.DMA((2, far, len(PIECES) + 1)),
            pltpu.SemaphoreType.DMA((2, far, len(PIECES))),
            pltpu.SemaphoreType.DMA((2, far, len(PIECES))),
            pltpu.SemaphoreType.DMA((plane,)),
            pltpu.SemaphoreType.DMA((plane,)),
            pltpu.SemaphoreType.DMA((plane,)),
            pltpu.SemaphoreType.DMA((plane,)),
            pltpu.SemaphoreType.DMA((metas,)),
            pltpu.SemaphoreType.DMA((metas,)),
            pltpu.SemaphoreType.DMA,
        ],
        compiler_params=pltpu.CompilerParams(
            collective_id=0, has_side_effects=True, vmem_limit_bytes=60 * 1024 * 1024
        ),
    )(values.reshape(values.shape[2:]), block_rows.reshape(1, CAP), block_cols.reshape(1, CAP))
    return purified.reshape(values.shape)


PLANES = {32: (4, 4), 8: (2, 2), 2: (1, 1)}


def solution(mesh):
    nx, ny = PLANES[mesh.shape["row"]]
    body = functools.partial(shards, nx, ny, mesh.shape["col"])
    in_specs = (P("row", "col", None, None, None), P("row", "col", None), P("row", "col", None))
    out_specs = P("row", "col", None, None, None)
    return jax.shard_map(body, mesh=mesh, in_specs=in_specs, out_specs=out_specs, check_vma=False)
```
